1024 devices in a mesh: grp: 8 (over x, core), clu: 128 (over z, y).
Axes of the slice: x: 4, y: 4, z: 32, core: 2. Of those that a mesh axis runs over, the one named last changes fastest.
Arguments:
- currents: bfloat16 [2, 262144, 128], P(None, ('grp', 'clu')), may hold values from -6 to 6
- live_slots: int32 [262144, 128], P(('grp', 'clu')), may hold values 0 or 1
- radiation: bfloat16 [2, 128, 128], replicated, may hold values from -0.5 to 0.5
- near_tiles: bfloat16 [2, 5, 128, 128], replicated, may hold values from -0.15625 to 0.15625
- leaf_transfer: float32 [2, 31, 128], replicated, may hold values from -1.5 to 1.5
- top_transfer: float32 [2, 31, 512], replicated, may hold values from -0.6 to 0.6
- interpolation: float32 [128, 512], replicated, may hold values from -0.5 to 0.5
- shift_angle: float32 [8, 512], replicated, may hold values from -3.140625 to 3.140625
Outputs:
- field: bfloat16 [2, 262144, 128], P(None, ('grp', 'clu'))
The draws below stay inside these ranges and needn't reach their ends.
All inputs are finite; a program needn't handle non-finite values. No bound on the sum of `live_slots` on one device may be relied on, other than what follows from the above.
Results may differ from the reference program's by a relative error of at most 0.0034.
The reference program's roundings to bfloat16 on the way (of `masked` and `incoming`) count: a program that leaves them out, or rounds other values in their place, can miss the bound.
Values may be sent and summed in bfloat16 or wider, within the bound.
No kernel may reach another device: no remote copies, remote signals or barrier semaphores. Data moves between devices by JAX's collectives and lax.ppermute only.
A program may use at most 64 MiB of HBM per device.

```python
import math
import jax
import jax.numpy as jnp
from jax import lax

B = 128
K1 = 128
K2 = 512
G = 8
NEAR = 2
LEAVES = 262144


def touch_ends(result, key, smallest, high):
    longest = result.shape.index(max(result.shape))
    spots = []
    for shift in (0, 1):
        where = [jax.random.randint(jax.random.fold_in(key, axis), (), 0, length) for axis, length in enumerate(result.shape)]
        where[longest] = (where[longest] + shift) % result.shape[longest]
        spots.append(tuple(where))
    return result.at[spots[0]].set(smallest).at[spots[1]].set(high)


def block_levels(own_key, extent, cuts, low, top_value):
    factor_of = 1.0
    for position, blocks in cuts:
        draws = jax.random.uniform(jax.random.fold_in(jax.random.fold_in(own_key, 6), position), (blocks,), jnp.float32, low / len(cuts), top_value / len(cuts))
        factor_of = factor_of * jnp.repeat(jnp.exp(draws), extent[position] // blocks).reshape((-1,) + (1,) * (len(extent) - 1 - position))
    return factor_of


def normal_values(stream_key, extent, scale, limit, split=(), kind=jnp.bfloat16):
    result = scale * jax.random.normal(stream_key, extent, jnp.float32)
    if split:
        result = result * block_levels(stream_key, extent, split, -0.22, 0.18)
    return jnp.clip(result, -limit, limit).astype(kind)


def setup_inputs(seed: int = 0) -> dict:
    key_list = jax.random.split(jax.random.key(seed), 9)
    return {
        "currents": normal_values(key_list[0], (2, LEAVES, B), 1.0, 6.0, ((1, 1024),)),
        "live_slots": touch_ends((jax.random.randint(key_list[1], (LEAVES, B), 0, 8) < 7).astype(jnp.int32), jax.random.fold_in(key_list[1], 1), 0, 1),
        "radiation": normal_values(key_list[2], (2, B, K1), B ** -0.5, 0.5),
        "near_tiles": normal_values(key_list[3], (2, 2 * NEAR + 1, B, B), (10 * B) ** -0.5, 0.15625),
        "leaf_transfer": normal_values(key_list[4], (2, 4 * G - 1, K1), 0.25, 1.5, (), jnp.float32),
        "top_transfer": normal_values(key_list[5], (2, 4 * G - 1, K2), 0.1, 0.6, (), jnp.float32),
        "interpolation": normal_values(key_list[6], (K1, K2), K1 ** -0.5, 0.5, (), jnp.float32),
        "shift_angle": jnp.clip(jax.random.uniform(key_list[7], (G, K2), jnp.float32, -3.140625, 3.140625), -3.140625, 3.140625),
    }


def complex_product(left, right):
    return jnp.stack([left[0] * right[0] - left[1] * right[1], left[0] * right[1] + left[1] * right[0]])

def complex_matmul(left, right):
    real_real = jnp.dot(left[0], right[0], preferred_element_type=jnp.float32)
    imag_imag = jnp.dot(left[1], right[1], preferred_element_type=jnp.float32)
    real_imag = jnp.dot(left[0], right[1], preferred_element_type=jnp.float32)
    imag_real = jnp.dot(left[1], right[0], preferred_element_type=jnp.float32)
    return jnp.stack([real_real - imag_imag, real_imag + imag_real])

def complex_receive(left, right):
    dims = (((1,), (1,)), ((), ()))
    real_real = lax.dot_general(left[0], right[0], dims, preferred_element_type=jnp.float32)
    imag_imag = lax.dot_general(left[1], right[1], dims, preferred_element_type=jnp.float32)
    imag_real = lax.dot_general(left[1], right[0], dims, preferred_element_type=jnp.float32)
    real_imag = lax.dot_general(left[0], right[1], dims, preferred_element_type=jnp.float32)
    return jnp.stack([real_real + imag_imag, imag_real - real_imag])

def displaced(array, offset):
    length = array.shape[1]
    if offset == 0:
        return array
    fill = jnp.zeros((array.shape[0], abs(offset)) + array.shape[2:], array.dtype)
    if offset > 0:
        return jnp.concatenate([fill, array[:, :length - offset]], axis=1)
    return jnp.concatenate([array[:, -offset:], fill], axis=1)

def adjacent(count, offset):
    index = jnp.arange(count, dtype=jnp.int32)
    return jnp.abs(index // G - (index - offset) // G) <= 1

def translate(patterns, table, nearest, reach):
    total = jnp.zeros(patterns.shape, jnp.float32)
    count = patterns.shape[1]
    for offset in range(-reach, reach + 1):
        if abs(offset) < nearest:
            continue
        term = complex_product(table[:, offset + reach][:, None, :], displaced(patterns, offset))
        total = total + jnp.where(adjacent(count, offset)[None, :, None], term, 0.0)
    return total

def reference(currents, live_slots, radiation, near_tiles, leaf_transfer, top_transfer, interpolation, shift_angle):
    highest = lax.Precision.HIGHEST
    masked = jnp.where(live_slots[None] == 1, currents, jnp.zeros((), jnp.bfloat16))
    near_field = jnp.zeros(currents.shape, jnp.float32)
    for offset in range(-NEAR, NEAR + 1):
        near_field = near_field + complex_matmul(displaced(masked, offset), near_tiles[:, offset + NEAR])
    leaf_patterns = complex_matmul(masked, radiation)
    reach = 2 * G - 1
    leaf_incoming = translate(leaf_patterns, leaf_transfer, NEAR + 1, reach)
    phase = jnp.stack([jnp.cos(shift_angle), jnp.sin(shift_angle)])
    conjugate = jnp.stack([jnp.cos(shift_angle), -jnp.sin(shift_angle)])
    parents = leaf_patterns.shape[1] // G
    block = math.gcd(parents, 4096)
    starts = jnp.arange(parents // block, dtype=jnp.int32) * block

    def aggregate(start):
        piece = lax.dynamic_slice_in_dim(leaf_patterns, start * G, block * G, 1)
        spread = jnp.einsum('snk,km->snm', piece, interpolation, precision=highest).reshape(2, block, G, -1)
        return lax.optimization_barrier(jnp.sum(complex_product(phase[:, None], spread), axis=2))
    top_patterns = jnp.moveaxis(lax.map(aggregate, starts), 0, 1).reshape(2, parents, -1)
    top_incoming = translate(top_patterns, top_transfer, 2, reach)

    def disaggregate(start):
        piece = lax.dynamic_slice_in_dim(top_incoming, start, block, 1)
        spread = complex_product(conjugate[:, None], piece[:, :, None, :]).reshape(2, block * G, -1)
        return jnp.einsum('snm,km->snk', spread, interpolation, precision=highest) * math.sqrt(K1 / K2)
    returned = jnp.moveaxis(lax.map(disaggregate, starts), 0, 1).reshape(2, parents * G, -1)
    incoming = (leaf_incoming + returned).astype(jnp.bfloat16)
    far_field = complex_receive(incoming, radiation)
    total = near_field + far_field
    return jnp.where(live_slots[None] == 1, total, 0.0).astype(jnp.bfloat16)
```

```python
import math

import jax
import jax.numpy as jnp
from jax import lax
from jax.experimental import pallas as pl
from jax.experimental.pallas import tpu as pltpu
from jax.sharding import PartitionSpec as P

G = 8
NEAR = 2
REACH = 2 * G - 1
HALO = G * G
F32 = jnp.float32
BF16 = jnp.bfloat16


def split(values):
    high = values.astype(BF16)
    return high, (values - high.astype(F32)).astype(BF16)


def paired(real, imag):
    return jnp.concatenate(
        [jnp.concatenate([real, imag], axis=1), jnp.concatenate([-imag, real], axis=1)], axis=0
    )


def mm(left, right):
    return jnp.dot(left, right, preferred_element_type=F32)


def mm_t(left, right):
    return lax.dot_general(left, right, (((1,), (1,)), ((), ())), preferred_element_type=F32)


def fill_table(table, transfer, nearest):
    width = transfer.shape[2]
    child = lax.broadcasted_iota(jnp.int32, (G, width), 0)
    for offset in range(-REACH, REACH + 1):
        if abs(offset) < nearest:
            continue
        index = offset + REACH
        real = jnp.broadcast_to(transfer[0, index : index + 1, :], (G, width))
        imag = jnp.broadcast_to(transfer[1, index : index + 1, :], (G, width))
        if offset > G:
            keep = child >= offset - G
        elif offset < -G:
            keep = child <= offset + REACH
        else:
            keep = None
        for part, value in enumerate((real, real + imag, imag - real)):
            table[index, part] = value if keep is None else jnp.where(keep, value, 0.0)


def translated(table, patterns, nearest, start, rows, lanes):
    sums = [jnp.zeros((rows // G, G, lanes.size), F32) for _ in range(3)]
    for offset in range(-REACH, REACH + 1):
        if abs(offset) < nearest:
            continue
        for part in range(3):
            source = patterns[part, pl.ds(start - offset, rows), lanes]
            factor = table[offset + REACH, part, :, lanes]
            sums[part] += factor[None] * source.reshape(rows // G, G, lanes.size)
    real = (sums[0] - sums[1]).reshape(rows, lanes.size)
    imag = (sums[0] + sums[2]).reshape(rows, lanes.size)
    return real, imag


def kernel(
    currents,
    live,
    lower,
    upper,
    radiation,
    tiles,
    leaf_transfer,
    top_transfer,
    interpolation,
    angle,
    field,
    x,
    leaf_table,
    top_table,
    leaf_pat,
    top_pat,
    top_in,
    spread_high,
    spread_low,
    incoming,
):
    count = currents.shape[1]
    k1 = radiation.shape[2]
    k2 = interpolation.shape[1]
    parents = count // G
    wide = parents + 2 * G
    keep = live[...] == 1
    for part in range(2):
        x[part, 0:HALO, :] = lower[part].astype(F32)
        x[part, HALO : HALO + count, :] = jnp.where(keep, currents[part].astype(F32), 0.0)
        x[part, HALO + count :, :] = upper[part].astype(F32)

    def cells(rows):
        return jnp.concatenate([x[0, rows, :], x[1, rows, :]], axis=1).astype(BF16)

    fill_table(leaf_table, leaf_transfer, NEAR + 1)
    fill_table(top_table, top_transfer, 2)
    matrix = paired(radiation[0], radiation[1])
    int_high, int_low = split(interpolation[...])
    cosine = jnp.cos(angle[...])
    sine = jnp.sin(angle[...])

    edge = 2 * G
    natural = mm(cells(pl.ds(HALO - edge, count + 2 * edge)), matrix)
    leaf_pat[0] = natural[:, :k1] + natural[:, k1:]
    leaf_pat[1] = natural[:, k1:]
    leaf_pat[2] = natural[:, :k1]

    ordered = jnp.concatenate([cells(pl.ds(c, wide, stride=G)) for c in range(G)], axis=0)
    by_child = mm(ordered, matrix)
    stacked = jnp.concatenate([by_child[:, :k1], by_child[:, k1:]], axis=0)
    high, low = split(stacked)
    both = jnp.concatenate([high, low], axis=1)
    twice = jnp.concatenate([int_high, int_high], axis=0)
    step = 256
    for begin in range(0, k2, step):
        cols = slice(begin, begin + step)
        spread = mm(both, twice[:, cols]) + mm(high, int_low[:, cols])
        real = jnp.zeros((wide, step), F32)
        imag = jnp.zeros((wide, step), F32)
        for c in range(G):
            sr = spread[c * wide : (c + 1) * wide]
            si = spread[(G + c) * wide : (G + c + 1) * wide]
            cc = cosine[c : c + 1, cols]
            ss = sine[c : c + 1, cols]
            real += cc * sr - ss * si
            imag += cc * si + ss * sr
        top_pat[0, G : G + wide, cols] = real + imag
        top_pat[1, G : G + wide, cols] = imag
        top_pat[2, G : G + wide, cols] = real
    for part in range(3):
        top_pat[part, 0:G, :] = jnp.zeros((G, k2), F32)
        top_pat[part, G + wide :, :] = jnp.zeros((G, k2), F32)

    for begin in range(0, k2, k1):
        lanes = pl.ds(begin, k1)
        real, imag = translated(top_table, top_pat, 2, 2 * G, parents, lanes)
        top_in[0, :, lanes] = real
        top_in[1, :, lanes] = imag

    block = 4 * G
    for begin in range(0, count, block):
        real, imag = translated(leaf_table, leaf_pat, NEAR + 1, edge + begin, block, pl.ds(0, k1))
        incoming[0, begin : begin + block, :] = real
        incoming[1, begin : begin + block, :] = imag

    for pair in range(0, parents, 2):
        reals, imags = [], []
        for p in (pair, pair + 1):
            tr = jnp.broadcast_to(top_in[0, p : p + 1, :], (G, k2))
            ti = jnp.broadcast_to(top_in[1, p : p + 1, :], (G, k2))
            reals.append(cosine * tr + sine * ti)
            imags.append(cosine * ti - sine * tr)
        for part, values in ((0, reals), (1, imags)):
            high, low = split(jnp.concatenate(values, axis=0))
            rows = pl.ds(part * count + pair * G, 2 * G)
            spread_high[rows, :] = high
            spread_low[rows, :] = low
    wide_back = mm_t(spread_high[...], jnp.concatenate([int_high, int_low], axis=0))
    back = wide_back[:, :k1] + wide_back[:, k1:] + mm_t(spread_low[...], int_high)
    back = back * math.sqrt(k1 / k2)
    gathered = jnp.concatenate(
        [
            (incoming[0] + back[:count]).astype(BF16),
            (incoming[1] + back[count:]).astype(BF16),
        ],
        axis=1,
    )
    total = mm_t(gathered, matrix)
    for offset in range(-NEAR, NEAR + 1):
        source = cells(pl.ds(HALO - offset, count))
        total += mm(source, paired(tiles[0, offset + NEAR], tiles[1, offset + NEAR]))
    field[0] = jnp.where(keep, total[:, :k1], 0.0).astype(BF16)
    field[1] = jnp.where(keep, total[:, k1:], 0.0).astype(BF16)


def shards(
    currents,
    live_slots,
    radiation,
    near_tiles,
    leaf_transfer,
    top_transfer,
    interpolation,
    shift_angle,
):
    count = currents.shape[1]
    k1 = radiation.shape[2]
    k2 = interpolation.shape[1]
    axis = ("grp", "clu")
    devices = lax.axis_size(axis)

    def edge(begin):
        cells = lax.slice_in_dim(currents, begin, begin + HALO, axis=1)
        alive = lax.slice_in_dim(live_slots, begin, begin + HALO, axis=0)
        return jnp.where(alive[None] == 1, cells, jnp.zeros((), BF16))

    lower = lax.ppermute(edge(count - HALO), axis, [(i, i + 1) for i in range(devices - 1)])
    upper = lax.ppermute(edge(0), axis, [(i + 1, i) for i in range(devices - 1)])
    wide = count // G + 2 * G
    offsets = 2 * REACH + 1
    return pl.pallas_call(
        kernel,
        out_shape=jax.ShapeDtypeStruct(currents.shape, BF16),
        scratch_shapes=[
            pltpu.VMEM((2, count + 2 * HALO, k1), F32),
            pltpu.VMEM((offsets, 3, G, k1), F32),
            pltpu.VMEM((offsets, 3, G, k2), F32),
            pltpu.VMEM((3, count + 4 * G, k1), F32),
            pltpu.VMEM((3, wide + 2 * G, k2), F32),
            pltpu.VMEM((2, count // G, k2), F32),
            pltpu.VMEM((2 * count, k2), BF16),
            pltpu.VMEM((2 * count, k2), BF16),
            pltpu.VMEM((2, count, k1), F32),
        ],
        compiler_params=pltpu.CompilerParams(vmem_limit_bytes=40 * 1024 * 1024),
        name="fmm",
    )(
        currents,
        live_slots,
        lower,
        upper,
        radiation,
        near_tiles,
        leaf_transfer,
        top_transfer,
        interpolation,
        shift_angle,
    )


def solution(mesh):
    in_specs = (
        P(None, ("grp", "clu"), None),
        P(("grp", "clu"), None),
        P(),
        P(),
        P(),
        P(),
        P(),
        P(),
    )
    out_specs = P(None, ("grp", "clu"), None)
    return jax.shard_map(shards, mesh=mesh, in_specs=in_specs, out_specs=out_specs, check_vma=False)
```

```python
import math

import jax
import jax.numpy as jnp
from jax import lax
from jax.experimental import pallas as pl
from jax.experimental.pallas import tpu as pltpu
from jax.sharding import PartitionSpec as P

G = 8
NEAR = 2
REACH = 2 * G - 1
HALO = G * G
PAD = 2 * G
F32 = jnp.float32
BF16 = jnp.bfloat16


def split(values):
    high = values.astype(BF16)
    return high, (values - high.astype(F32)).astype(BF16)


def paired(real, imag):
    return jnp.concatenate(
        [jnp.concatenate([real, imag], axis=1), jnp.concatenate([-imag, real], axis=1)], axis=0
    )


def mm(left, right):
    return jnp.dot(left, right, preferred_element_type=F32)


def mm_t(left, right):
    return lax.dot_general(left, right, (((1,), (1,)), ((), ())), preferred_element_type=F32)


def cells(x, rows):
    return jnp.concatenate([x[0, rows, :], x[1, rows, :]], axis=1).astype(BF16)


def fill_table(table, transfer, nearest):
    width = transfer.shape[2]
    child = lax.broadcasted_iota(jnp.int32, (G, width), 0)
    for offset in range(-REACH, REACH + 1):
        if abs(offset) < nearest:
            continue
        index = offset + REACH
        real = jnp.broadcast_to(transfer[index, 0:1, :], (G, width))
        imag = jnp.broadcast_to(transfer[index, 1:2, :], (G, width))
        if offset > G:
            keep = child >= offset - G
        elif offset < -G:
            keep = child <= offset + REACH
        else:
            keep = None
        for part, value in enumerate((real, real + imag, imag - real)):
            table[index, part] = value if keep is None else jnp.where(keep, value, 0.0)


def translated(table, patterns, offsets, start, rows, lanes):
    sums = [jnp.zeros((rows // G, G, lanes.size), F32) for _ in range(3)]
    for offset in offsets:
        for part in range(3):
            source = patterns[part, pl.ds(start - offset, rows), lanes]
            factor = table[offset + REACH, part, :, lanes]
            sums[part] += factor[None] * source.reshape(rows // G, G, lanes.size)
    real = (sums[0] - sums[1]).reshape(rows, lanes.size)
    imag = (sums[0] + sums[2]).reshape(rows, lanes.size)
    return real, imag


def offsets_of(nearest):
    return [d for d in range(-REACH, REACH + 1) if abs(d) >= nearest]


def store_patterns(patterns, rows, lanes, real, imag):
    patterns[0, rows, lanes] = real + imag
    patterns[1, rows, lanes] = imag
    patterns[2, rows, lanes] = real


def aggregated(by_child, parents, weights, cosine, sine, store):
    k1, k2 = weights.shape[0] // 2, weights.shape[1]
    stacked = jnp.concatenate([by_child[:, :k1], by_child[:, k1:]], axis=0)
    high, low = split(stacked)
    both = jnp.concatenate([high, low], axis=1)
    step = 256
    for begin in range(0, k2, step):
        cols = slice(begin, begin + step)
        int_high = weights[:k1, cols]
        twice = jnp.concatenate([int_high, int_high], axis=0)
        spread = mm(both, twice) + mm(high, weights[k1:, cols])
        real = jnp.zeros((parents, step), F32)
        imag = jnp.zeros((parents, step), F32)
        for c in range(G):
            sr = spread[c * parents : (c + 1) * parents]
            si = spread[(G + c) * parents : (G + c + 1) * parents]
            cc = cosine[c : c + 1, cols]
            ss = sine[c : c + 1, cols]
            real += cc * sr - ss * si
            imag += cc * si + ss * sr
        store(cols, real, imag)


def disaggregated(top_in, first, parents, weights, cosine, sine, spread_high, spread_low):
    k1, k2 = weights.shape[0] // 2, weights.shape[1]
    rows_each = parents * G
    for pair in range(0, parents, 2):
        reals, imags = [], []
        for p in (first + pair, first + pair + 1):
            tr = jnp.broadcast_to(top_in[0, p : p + 1, :], (G, k2))
            ti = jnp.broadcast_to(top_in[1, p : p + 1, :], (G, k2))
            reals.append(cosine[...] * tr + sine[...] * ti)
            imags.append(cosine[...] * ti - sine[...] * tr)
        for part, values in ((0, reals), (1, imags)):
            high, low = split(jnp.concatenate(values, axis=0))
            rows = pl.ds(part * rows_each + pair * G, 2 * G)
            spread_high[rows, :] = high
            spread_low[rows, :] = low
    wide = mm_t(spread_high[...], weights[...])
    back = wide[:, :k1] + wide[:, k1:] + mm_t(spread_low[...], weights[:k1])
    back = back * math.sqrt(k1 / k2)
    return back[:rows_each], back[rows_each:]


def local_part(inputs, state, work):
    hbm, staged, sems = inputs
    copies = [pltpu.make_async_copy(a, b, sems.at[i]) for i, (a, b) in enumerate(zip(hbm, staged))]
    for copy in copies:
        copy.start()
    for copy in copies:
        copy.wait()
    currents, live, radiation, tiles, leaf_transfer, top_transfer, interpolation, angle = staged
    (
        middle,
        near_edge,
        leaf_edge,
        top_edge,
        live_edge,
        matrix,
        near,
        weights,
        cosine,
        sine,
        leaf_table,
        top_table,
    ) = state
    x, leaf_pat, top_pat, top_in, spread_high, spread_low, incoming = work
    count = currents.shape[1]
    k1 = radiation.shape[2]
    k2 = interpolation.shape[1]
    parents = count // G
    keep = live[...] == 1
    for part in range(2):
        x[part, 0:PAD, :] = jnp.zeros((PAD, k1), F32)
        x[part, PAD : PAD + count, :] = jnp.where(keep, currents[part].astype(F32), 0.0)
        x[part, PAD + count :, :] = jnp.zeros((PAD, k1), F32)
    live_edge[0:HALO] = live[0:HALO]
    live_edge[HALO:] = live[count - HALO :]
    fill_table(leaf_table, leaf_transfer, NEAR + 1)
    fill_table(top_table, top_transfer, 2)
    matrix[...] = paired(radiation[0], radiation[1])
    for index in range(2 * NEAR + 1):
        near[index] = paired(tiles[0, index], tiles[1, index])
    int_high, int_low = split(interpolation[...])
    weights[:k1] = int_high
    weights[k1:] = int_low
    cosine[...] = jnp.cos(angle[...])
    sine[...] = jnp.sin(angle[...])

    natural = mm(cells(x, pl.ds(0, count + 2 * PAD)), matrix[...])
    store_patterns(leaf_pat, slice(None), slice(None), natural[:, :k1], natural[:, k1:])
    ordered = [cells(x, pl.ds(PAD + c, parents, stride=G)) for c in range(G)]
    by_child = mm(jnp.concatenate(ordered, axis=0), matrix[...])

    def store(cols, real, imag):
        store_patterns(top_pat, pl.ds(PAD, parents), cols, real, imag)

    aggregated(by_child, parents, weights, cosine, sine, store)
    for part in range(3):
        top_pat[part, 0:PAD, :] = jnp.zeros((PAD, k2), F32)
        top_pat[part, PAD + parents :, :] = jnp.zeros((PAD, k2), F32)
    for begin in range(0, k2, k1):
        lanes = pl.ds(begin, k1)
        sums = translated(top_table, top_pat, offsets_of(2), PAD, parents, lanes)
        for part in range(2):
            top_in[part, :, lanes] = sums[part]
            top_edge[part, 0:G, lanes] = sums[part][:G]
            top_edge[part, G:, lanes] = sums[part][parents - G :]
    block = 4 * G
    for begin in range(0, count, block):
        sums = translated(
            leaf_table, leaf_pat, offsets_of(NEAR + 1), PAD + begin, block, pl.ds(0, k1)
        )
        for part in range(2):
            incoming[part, begin : begin + block, :] = sums[part]
    for part in range(2):
        leaf_edge[part, 0:HALO] = incoming[part, 0:HALO]
        leaf_edge[part, HALO:] = incoming[part, count - HALO :]

    total = jnp.zeros((count, 2 * k1), F32)
    for offset in range(-NEAR, NEAR + 1):
        total += mm(cells(x, pl.ds(PAD - offset, count)), near[offset + NEAR])
    near_edge[0:HALO] = total[:HALO]
    near_edge[HALO:] = total[count - HALO :]

    inside = slice(HALO, count - HALO)
    back = disaggregated(
        top_in, G, parents - 2 * G, weights, cosine, sine, spread_high, spread_low
    )
    gathered = jnp.concatenate(
        [(incoming[part, inside] + back[part]).astype(BF16) for part in range(2)], axis=1
    )
    field = mm_t(gathered, matrix[...]) + total[inside]
    for part in range(2):
        values = field[:, part * k1 : (part + 1) * k1]
        middle[part] = jnp.where(keep[inside], values, 0.0).astype(BF16)


def position():
    clu = lax.axis_index("clu")
    leads = jnp.logical_and(clu == 0, lax.axis_index("grp") > 0)
    return lax.rem(clu, 2), jnp.logical_or(leads, clu == 1)


def first_kernel(*refs):
    hbm = refs[:8]
    send_cross, send_inner = refs[8:10]
    state = refs[10:22]
    edge, alive, edge_sems = refs[22:25]
    staged, sems, work = refs[25:33], refs[33], refs[34:]
    currents, live = hbm[:2]
    count = currents.shape[1]
    odd, early = position()
    copies = []
    for side, rows in enumerate((pl.ds(0, HALO), pl.ds(count - HALO, HALO))):
        copies.append(
            pltpu.make_async_copy(currents.at[:, rows, :], edge.at[side], edge_sems.at[side])
        )
        copies.append(
            pltpu.make_async_copy(live.at[rows, :], alive.at[side], edge_sems.at[2 + side])
        )
    for copy in copies:
        copy.start()
    for copy in copies:
        copy.wait()
    for send, side in ((send_cross, odd), (send_inner, 1 - odd)):
        keep = alive[side] == 1
        for part in range(2):
            values = edge[side, part].astype(F32)
            send[part] = jnp.where(keep, values, 0.0).astype(BF16)

    @pl.when(early)
    def _():
        local_part((hbm, staged, sems), state, work)


def last_kernel(*refs):
    hbm = refs[:8]
    received = refs[8:11]
    state = refs[11:23]
    field = refs[23]
    late_state = refs[24:36]
    staged, sems, work = refs[36:44], refs[44], refs[45:52]
    odd, early = position()

    @pl.when(early)
    def _():
        outer_part(received, odd, state, field, refs[52:])

    @pl.when(jnp.logical_not(early))
    def _():
        local_part((hbm, staged, sems), late_state, work)
        outer_part(received, odd, late_state, field, refs[52:])


def outer_part(received, odd, state, field, work):
    (
        middle,
        near_edge,
        leaf_edge,
        top_edge,
        live_edge,
        matrix,
        near,
        weights,
        cosine,
        sine,
        leaf_table,
        top_table,
    ) = state
    cross, inner, inner_late = received
    halo, near_pad, leaf_pad, top_pad, top_sum, edge_high, edge_low, out, out_sems = work
    count = field.shape[1]
    k1 = matrix.shape[0] // 2
    k2 = weights.shape[1]
    inside = pl.ds(HALO, count - 2 * HALO)
    out[:, inside, :] = middle[...]
    middle_copy = pltpu.make_async_copy(
        out.at[:, inside, :], field.at[:, inside, :], out_sems.at[2]
    )
    middle_copy.start()

    for part in range(2):
        halo[part, pl.ds(pl.multiple_of(odd * HALO, HALO), HALO), :] = cross[part].astype(F32)
        halo[part, pl.ds(pl.multiple_of((1 - odd) * HALO, HALO), HALO), :] = inner[part].astype(
            F32
        ) + inner_late[part].astype(F32)
    ordered = [cells(halo, pl.ds(c, 2 * G, stride=G)) for c in range(G)]
    ordered.append(cells(halo, pl.ds(HALO - PAD, 2 * PAD)))
    patterns = mm(jnp.concatenate(ordered, axis=0), matrix[...])

    for part in range(3):
        for side in range(2):
            for begin in (0, 2 * G):
                top_pad[side, part, begin : begin + G, :] = jnp.zeros((G, k2), F32)
                leaf_pad[side, part, begin : begin + G, :] = jnp.zeros((G, k1), F32)

    def store(cols, real, imag):
        for side in range(2):
            rows = slice(side * G, (side + 1) * G)
            store_patterns(top_pad.at[side], pl.ds(G, G), cols, real[rows], imag[rows])

    aggregated(patterns[: 2 * HALO], 2 * G, weights, cosine, sine, store)
    before = lambda nearest: [d for d in offsets_of(nearest) if d > 0]
    after = lambda nearest: [d for d in offsets_of(nearest) if d < 0]
    for side, offsets, start in ((0, before(2), 2 * G), (1, after(2), 0)):
        rows = slice(side * G, (side + 1) * G)
        for begin in range(0, k2, k1):
            lanes = pl.ds(begin, k1)
            sums = translated(top_table, top_pad.at[side], offsets, start, G, lanes)
            for part in range(2):
                top_sum[part, rows, lanes] = top_edge[part, rows, lanes] + sums[part]

    last = 2 * HALO
    leaf_sums = []
    for side, offsets, start in ((0, before(NEAR + 1), 2 * G), (1, after(NEAR + 1), 0)):
        rows = slice(last + G + side * G, last + 2 * G + side * G)
        store_patterns(
            leaf_pad.at[side], pl.ds(G, G), slice(None), patterns[rows, :k1], patterns[rows, k1:]
        )
        leaf_sums.append(
            translated(leaf_table, leaf_pad.at[side], offsets, start, G, pl.ds(0, k1))
        )

    back = disaggregated(top_sum, 0, 2 * G, weights, cosine, sine, edge_high, edge_low)
    parts = []
    for part in range(2):
        blank = jnp.zeros((last - 2 * G, k1), F32)
        extra = jnp.concatenate([leaf_sums[0][part], blank, leaf_sums[1][part]], axis=0)
        parts.append((leaf_edge[part] + extra + back[part]).astype(BF16))
    total = mm_t(jnp.concatenate(parts, axis=1), matrix[...]) + near_edge[...]

    for part in range(2):
        near_pad[0, part] = jnp.zeros((4 * G, k1), F32)
        near_pad[1, part] = jnp.zeros((4 * G, k1), F32)
        near_pad[0, part, G : 2 * G, :] = halo[part, HALO - G : HALO, :]
        near_pad[1, part, 3 * G :, :] = halo[part, HALO : HALO + G, :]
    head = jnp.zeros((PAD, 2 * k1), F32)
    tail = jnp.zeros((PAD, 2 * k1), F32)
    for offset in range(1, NEAR + 1):
        head += mm(cells(near_pad.at[0], pl.ds(2 * G - offset, PAD)), near[NEAR + offset])
        tail += mm(cells(near_pad.at[1], pl.ds(G + offset, PAD)), near[NEAR - offset])
    blank = jnp.zeros((last - 2 * PAD, 2 * k1), F32)
    total = total + jnp.concatenate([head, blank, tail], axis=0)
    keep = live_edge[...] == 1
    for part in range(2):
        values = total[:, part * k1 : (part + 1) * k1]
        values = jnp.where(keep, values, 0.0).astype(BF16)
        out[part, 0:HALO, :] = values[:HALO]
        out[part, count - HALO :, :] = values[HALO:]
    copies = []
    for side, begin in enumerate((0, count - HALO)):
        rows = pl.ds(begin, HALO)
        copies.append(
            pltpu.make_async_copy(
                out.at[:, rows, :], field.at[:, rows, :], out_sems.at[side]
            )
        )
    for copy in copies:
        copy.start()
    for copy in copies:
        copy.wait()
    middle_copy.wait()


def shards(
    currents,
    live_slots,
    radiation,
    near_tiles,
    leaf_transfer,
    top_transfer,
    interpolation,
    shift_angle,
):
    count = currents.shape[1]
    k1 = radiation.shape[2]
    k2 = interpolation.shape[1]
    parents = count // G
    offsets = 2 * REACH + 1
    edge = 2 * HALO
    axis = ("grp", "clu")
    region = lax.axis_size("clu")
    devices = lax.axis_size(axis)
    shape = jax.ShapeDtypeStruct
    hbm = pl.BlockSpec(memory_space=pltpu.HBM)
    vmem = pl.BlockSpec(memory_space=pltpu.VMEM)
    arrays = (
        currents,
        live_slots,
        radiation,
        near_tiles,
        jnp.swapaxes(leaf_transfer, 0, 1),
        jnp.swapaxes(top_transfer, 0, 1),
        interpolation,
        shift_angle,
    )
    arrays = [pltpu.with_memory_space_constraint(a, pltpu.HBM) for a in arrays]
    state = (
        shape((2, count - edge, k1), BF16),
        shape((edge, 2 * k1), F32),
        shape((2, edge, k1), F32),
        shape((2, 2 * G, k2), F32),
        shape((edge, k1), jnp.int32),
        shape((2 * k1, 2 * k1), BF16),
        shape((2 * NEAR + 1, 2 * k1, 2 * k1), BF16),
        shape((2 * k1, k2), BF16),
        shape((G, k2), F32),
        shape((G, k2), F32),
        shape((offsets, 3, G, k1), F32),
        shape((offsets, 3, G, k2), F32),
    )
    local_scratch = [pltpu.VMEM(a.shape, a.dtype) for a in arrays] + [
        pltpu.SemaphoreType.DMA((len(arrays),)),
        pltpu.VMEM((2, count + 2 * PAD, k1), F32),
        pltpu.VMEM((3, count + 2 * PAD, k1), F32),
        pltpu.VMEM((3, parents + 2 * PAD, k2), F32),
        pltpu.VMEM((2, parents, k2), F32),
        pltpu.VMEM((2 * (count - edge), k2), BF16),
        pltpu.VMEM((2 * (count - edge), k2), BF16),
        pltpu.VMEM((2, count, k1), F32),
    ]
    send = shape((2, HALO, k1), BF16)
    params = pltpu.CompilerParams(vmem_limit_bytes=24 * 1024 * 1024)
    send_cross, send_inner, *kept = pl.pallas_call(
        first_kernel,
        out_shape=(send, send) + state,
        in_specs=[hbm] * len(arrays),
        out_specs=(vmem,) * (2 + len(state)),
        scratch_shapes=[
            pltpu.VMEM((2, 2, HALO, k1), BF16),
            pltpu.VMEM((2, HALO, k1), jnp.int32),
            pltpu.SemaphoreType.DMA((4,)),
        ]
        + local_scratch,
        compiler_params=params,
        name="edges_and_early_local",
    )(*arrays)

    def swaps(values, begin, keep):
        pairs = [(i, i + 1) for i in range(begin, devices - 1, 2) if keep(i)]
        return lax.ppermute(values, axis, pairs + [(j, i) for i, j in pairs])

    def leads(i):
        return i > 0 and i % region == 0

    inner = swaps(send_inner, 0, leads)
    send_cross, send_inner, inner = lax.optimization_barrier((send_cross, send_inner, inner))
    cross = swaps(send_cross, 1, lambda i: True)
    inner_late = swaps(send_inner, 0, lambda i: not leads(i))
    return pl.pallas_call(
        last_kernel,
        out_shape=shape(currents.shape, BF16),
        in_specs=[hbm] * len(arrays) + [vmem] * (3 + len(state)),
        out_specs=hbm,
        scratch_shapes=[pltpu.VMEM(a.shape, a.dtype) for a in state]
        + local_scratch
        + [
            pltpu.VMEM((2, edge, k1), F32),
            pltpu.VMEM((2, 2, 4 * G, k1), F32),
            pltpu.VMEM((2, 3, 3 * G, k1), F32),
            pltpu.VMEM((2, 3, 3 * G, k2), F32),
            pltpu.VMEM((2, 2 * G, k2), F32),
            pltpu.VMEM((2 * edge, k2), BF16),
            pltpu.VMEM((2 * edge, k2), BF16),
            pltpu.VMEM((2, count, k1), BF16),
            pltpu.SemaphoreType.DMA((3,)),
        ],
        compiler_params=params,
        name="late_local_and_halo",
    )(*arrays, cross, inner, inner_late, *kept)


def solution(mesh):
    in_specs = (
        P(None, ("grp", "clu"), None),
        P(("grp", "clu"), None),
        P(),
        P(),
        P(),
        P(),
        P(),
        P(),
    )
    out_specs = P(None, ("grp", "clu"), None)
    return jax.shard_map(shards, mesh=mesh, in_specs=in_specs, out_specs=out_specs, check_vma=False)
```

```python
import math

import jax
import jax.numpy as jnp
from jax import lax
from jax.experimental import pallas as pl
from jax.experimental.pallas import tpu as pltpu
from jax.sharding import PartitionSpec as P

G = 8
NEAR = 2
REACH = 2 * G - 1
HALO = G * G
PAD = 2 * G
F32 = jnp.float32
BF16 = jnp.bfloat16


def split(values):
    high = values.astype(BF16)
    return high, (values - high.astype(F32)).astype(BF16)


def paired(real, imag):
    return jnp.concatenate(
        [jnp.concatenate([real, imag], axis=1), jnp.concatenate([-imag, real], axis=1)], axis=0
    )


def mm(left, right):
    return jnp.dot(left, right, preferred_element_type=F32)


def mm_t(left, right):
    return lax.dot_general(left, right, (((1,), (1,)), ((), ())), preferred_element_type=F32)


def cells(x, rows):
    return jnp.concatenate([x[0, rows, :], x[1, rows, :]], axis=1).astype(BF16)


def fill_table(table, transfer, nearest):
    width = transfer.shape[2]
    child = lax.broadcasted_iota(jnp.int32, (G, width), 0)
    for offset in range(-REACH, REACH + 1):
        if abs(offset) < nearest:
            continue
        index = offset + REACH
        real = jnp.broadcast_to(transfer[index, 0:1, :], (G, width))
        imag = jnp.broadcast_to(transfer[index, 1:2, :], (G, width))
        if offset > G:
            keep = child >= offset - G
        elif offset < -G:
            keep = child <= offset + REACH
        else:
            keep = None
        for part, value in enumerate((real, real + imag, imag - real)):
            table[index, part] = value if keep is None else jnp.where(keep, value, 0.0)


def translated(table, patterns, offsets, start, rows, lanes):
    sums = [jnp.zeros((rows // G, G, lanes.size), F32) for _ in range(3)]
    for offset in offsets:
        for part in range(3):
            source = patterns[part, pl.ds(start - offset, rows), lanes]
            factor = table[offset + REACH, part, :, lanes]
            sums[part] += factor[None] * source.reshape(rows // G, G, lanes.size)
    real = (sums[0] - sums[1]).reshape(rows, lanes.size)
    imag = (sums[0] + sums[2]).reshape(rows, lanes.size)
    return real, imag


def offsets_of(nearest):
    return [d for d in range(-REACH, REACH + 1) if abs(d) >= nearest]


def store_patterns(patterns, rows, lanes, real, imag):
    patterns[0, rows, lanes] = real + imag
    patterns[1, rows, lanes] = imag
    patterns[2, rows, lanes] = real


def aggregated(by_child, parents, weights, cosine, sine, store):
    k1, k2 = weights.shape[0] // 2, weights.shape[1]
    stacked = jnp.concatenate([by_child[:, :k1], by_child[:, k1:]], axis=0)
    high, low = split(stacked)
    both = jnp.concatenate([high, low], axis=1)
    step = 256
    for begin in range(0, k2, step):
        cols = slice(begin, begin + step)
        int_high = weights[:k1, cols]
        twice = jnp.concatenate([int_high, int_high], axis=0)
        spread = mm(both, twice) + mm(high, weights[k1:, cols])
        real = jnp.zeros((parents, step), F32)
        imag = jnp.zeros((parents, step), F32)
        for c in range(G):
            sr = spread[c * parents : (c + 1) * parents]
            si = spread[(G + c) * parents : (G + c + 1) * parents]
            cc = cosine[c : c + 1, cols]
            ss = sine[c : c + 1, cols]
            real += cc * sr - ss * si
            imag += cc * si + ss * sr
        store(cols, real, imag)


def disaggregated(top_in, first, parents, weights, cosine, sine, spread_high, spread_low):
    k1, k2 = weights.shape[0] // 2, weights.shape[1]
    rows_each = parents * G
    for pair in range(0, parents, 2):
        reals, imags = [], []
        for p in (first + pair, first + pair + 1):
            tr = jnp.broadcast_to(top_in[0, p : p + 1, :], (G, k2))
            ti = jnp.broadcast_to(top_in[1, p : p + 1, :], (G, k2))
            reals.append(cosine[...] * tr + sine[...] * ti)
            imags.append(cosine[...] * ti - sine[...] * tr)
        for part, values in ((0, reals), (1, imags)):
            high, low = split(jnp.concatenate(values, axis=0))
            rows = pl.ds(part * rows_each + pair * G, 2 * G)
            spread_high[rows, :] = high
            spread_low[rows, :] = low
    wide = mm_t(spread_high[...], weights[...])
    back = wide[:, :k1] + wide[:, k1:] + mm_t(spread_low[...], weights[:k1])
    back = back * math.sqrt(k1 / k2)
    return back[:rows_each], back[rows_each:]


def local_part(inputs, state, work):
    hbm, staged, sems = inputs
    copies = [pltpu.make_async_copy(a, b, sems.at[i]) for i, (a, b) in enumerate(zip(hbm, staged))]
    for copy in copies:
        copy.start()
    for copy in copies:
        copy.wait()
    currents, live, radiation, tiles, leaf_transfer, top_transfer, interpolation, angle = staged
    (
        middle,
        near_edge,
        leaf_edge,
        top_edge,
        live_edge,
        matrix,
        near,
        weights,
        cosine,
        sine,
        combined,
        leaf_table,
        top_table,
    ) = state
    x, leaf_pat, top_pat, top_in, spread_high, spread_low, incoming = work
    count = currents.shape[1]
    k1 = radiation.shape[2]
    k2 = interpolation.shape[1]
    parents = count // G
    keep = live[...] == 1
    for part in range(2):
        x[part, 0:PAD, :] = jnp.zeros((PAD, k1), F32)
        x[part, PAD : PAD + count, :] = jnp.where(keep, currents[part].astype(F32), 0.0)
        x[part, PAD + count :, :] = jnp.zeros((PAD, k1), F32)
    live_edge[0:HALO] = live[0:HALO]
    live_edge[HALO:] = live[count - HALO :]
    fill_table(leaf_table, leaf_transfer, NEAR + 1)
    fill_table(top_table, top_transfer, 2)
    matrix[...] = paired(radiation[0], radiation[1])
    for index in range(2 * NEAR + 1):
        near[index] = paired(tiles[0, index], tiles[1, index])
    int_high, int_low = split(interpolation[...])
    weights[:k1] = int_high
    weights[k1:] = int_low
    cosine[...] = jnp.cos(angle[...])
    sine[...] = jnp.sin(angle[...])
    for part in range(2):
        half = matrix[:, part * k1 : (part + 1) * k1]
        high, low = split(mm(half, int_high) + mm(half, int_low))
        combined[0, :, part * k2 : (part + 1) * k2] = high
        combined[1, :, part * k2 : (part + 1) * k2] = low

    natural = mm(cells(x, pl.ds(0, count + 2 * PAD)), matrix[...])
    store_patterns(leaf_pat, slice(None), slice(None), natural[:, :k1], natural[:, k1:])
    ordered = [cells(x, pl.ds(PAD + c, parents, stride=G)) for c in range(G)]
    by_child = mm(jnp.concatenate(ordered, axis=0), matrix[...])

    def store(cols, real, imag):
        store_patterns(top_pat, pl.ds(PAD, parents), cols, real, imag)

    aggregated(by_child, parents, weights, cosine, sine, store)
    for part in range(3):
        top_pat[part, 0:PAD, :] = jnp.zeros((PAD, k2), F32)
        top_pat[part, PAD + parents :, :] = jnp.zeros((PAD, k2), F32)
    for begin in range(0, k2, k1):
        lanes = pl.ds(begin, k1)
        sums = translated(top_table, top_pat, offsets_of(2), PAD, parents, lanes)
        for part in range(2):
            top_in[part, :, lanes] = sums[part]
            top_edge[part, 0:G, lanes] = sums[part][:G]
            top_edge[part, G:, lanes] = sums[part][parents - G :]
    block = 4 * G
    for begin in range(0, count, block):
        sums = translated(
            leaf_table, leaf_pat, offsets_of(NEAR + 1), PAD + begin, block, pl.ds(0, k1)
        )
        for part in range(2):
            incoming[part, begin : begin + block, :] = sums[part]
    for part in range(2):
        leaf_edge[part, 0:HALO] = incoming[part, 0:HALO]
        leaf_edge[part, HALO:] = incoming[part, count - HALO :]

    total = jnp.zeros((count, 2 * k1), F32)
    for offset in range(-NEAR, NEAR + 1):
        total += mm(cells(x, pl.ds(PAD - offset, count)), near[offset + NEAR])
    near_edge[0:HALO] = total[:HALO]
    near_edge[HALO:] = total[count - HALO :]

    inside = slice(HALO, count - HALO)
    back = disaggregated(
        top_in, G, parents - 2 * G, weights, cosine, sine, spread_high, spread_low
    )
    gathered = jnp.concatenate(
        [(incoming[part, inside] + back[part]).astype(BF16) for part in range(2)], axis=1
    )
    field = mm_t(gathered, matrix[...]) + total[inside]
    for part in range(2):
        values = field[:, part * k1 : (part + 1) * k1]
        middle[part] = jnp.where(keep[inside], values, 0.0).astype(BF16)


def position():
    clu = lax.axis_index("clu")
    leads = jnp.logical_and(clu == 0, lax.axis_index("grp") > 0)
    return lax.rem(clu, 2), leads


def lead_kernel(*refs):
    hbm, send, state = refs[:8], refs[8], refs[9:22]
    alive, edge_sems = refs[22:24]
    staged, sems, work = refs[24:32], refs[32], refs[33:]
    odd, leads = position()

    @pl.when(jnp.logical_and(lax.axis_index("clu") < 2, lax.axis_index("grp") > 0))
    def _():
        currents, live = hbm[:2]
        begin = (1 - odd) * (currents.shape[1] - HALO)
        rows = pl.ds(pl.multiple_of(begin, HALO), HALO)
        copies = [
            pltpu.make_async_copy(currents.at[:, rows, :], send, edge_sems.at[0]),
            pltpu.make_async_copy(live.at[rows, :], alive, edge_sems.at[1]),
        ]
        for copy in copies:
            copy.start()
        for copy in copies:
            copy.wait()
        mask(send, send, alive[...])

    @pl.when(leads)
    def _():
        local_part((hbm, staged, sems), state, work)


def mask(target, source, alive):
    for part in range(2):
        target[part] = jnp.where(alive == 1, source[part].astype(F32), 0.0).astype(BF16)


def edge_kernel(currents, live, after, cross, inner):
    odd, _ = position()
    begin = currents.shape[1] - HALO
    for target, side in ((cross, odd), (inner, 1 - odd)):
        rows = pl.ds(pl.multiple_of(side * begin, HALO), HALO)
        mask(target, currents.at[:, rows, :], live[rows, :])


def inner_kernel(*refs):
    inner, state, rows = refs[0], refs[1:14], refs[16]
    halo, *work = refs[17:]
    odd, leads = position()

    @pl.when(leads)
    def _():
        for part in range(2):
            halo[part, HALO:, :] = inner[part].astype(F32)
        outer_part(halo, (1,), state, (rows,), work)


def last_kernel(*refs):
    hbm = refs[:8]
    cross, inner, inner_late, inner_rows = refs[8:12]
    state = refs[12:25]
    field = refs[25]
    late_state = refs[26:39]
    staged, sems, local_work = refs[39:47], refs[47], refs[48:55]
    lower, upper, out_sems, halo, *work = refs[55:]
    count = field.shape[1]
    inside = pl.ds(HALO, count - 2 * HALO)
    head, tail = pl.ds(0, HALO), pl.ds(count - HALO, HALO)
    odd, leads = position()

    def sent(source, rows, index):
        copy = pltpu.make_async_copy(source, field.at[:, rows, :], out_sems.at[index])
        copy.start()
        return copy

    @pl.when(leads)
    def _():
        copies = [sent(state[0], inside, 0), sent(inner_rows, tail, 1)]
        for part in range(2):
            halo[part, 0:HALO, :] = cross[part].astype(F32)
        outer_part(halo, (0,), state, (lower,), work)
        copies.append(sent(lower, head, 2))
        for copy in copies:
            copy.wait()

    @pl.when(jnp.logical_not(leads))
    def _():
        local_part((hbm, staged, sems), late_state, local_work)
        copies = [sent(late_state[0], inside, 0)]
        for part in range(2):
            halo[part, pl.ds(pl.multiple_of(odd * HALO, HALO), HALO), :] = cross[part].astype(F32)
            halo[part, pl.ds(pl.multiple_of((1 - odd) * HALO, HALO), HALO), :] = inner[
                part
            ].astype(F32) + inner_late[part].astype(F32)
        outer_part(halo, (0, 1), late_state, (lower, upper), work)
        copies += [sent(upper, tail, 1), sent(lower, head, 2)]
        for copy in copies:
            copy.wait()


def outer_part(halo, sides, state, fields, work):
    (
        middle,
        near_edge,
        leaf_edge,
        top_edge,
        live_edge,
        matrix,
        near,
        weights,
        cosine,
        sine,
        combined,
        leaf_table,
        top_table,
    ) = state
    near_pad, leaf_pad, top_pad, top_sum, edge_high, edge_low = work
    k1 = matrix.shape[0] // 2
    k2 = weights.shape[1]
    rows_of = [slice(side * HALO, (side + 1) * HALO) for side in sides]
    wide = len(sides) * G

    def both(rows):
        return jnp.concatenate([halo[0, rows, :], halo[1, rows, :]], axis=1)

    ordered = [both(pl.ds(side * HALO + c, G, stride=G)) for c in range(G) for side in sides]
    ordered = jnp.concatenate(ordered, axis=0).astype(BF16)
    for part in range(3):
        for side in sides:
            for begin in (0, 2 * G):
                top_pad[side, part, begin : begin + G, :] = jnp.zeros((G, k2), F32)
                leaf_pad[side, part, begin : begin + G, :] = jnp.zeros((G, k1), F32)
    step = 256
    for begin in range(0, k2, step):
        cols = slice(begin, begin + step)
        spread = []
        for first in (begin, k2 + begin):
            taken = slice(first, first + step)
            spread.append(mm(ordered, combined[0, :, taken]) + mm(ordered, combined[1, :, taken]))
        real = jnp.zeros((wide, step), F32)
        imag = jnp.zeros((wide, step), F32)
        for c in range(G):
            sr, si = [value[c * wide : (c + 1) * wide] for value in spread]
            cc = cosine[c : c + 1, cols]
            ss = sine[c : c + 1, cols]
            real += cc * sr - ss * si
            imag += cc * si + ss * sr
        for at, side in enumerate(sides):
            rows = slice(at * G, (at + 1) * G)
            store_patterns(top_pad.at[side], pl.ds(G, G), cols, real[rows], imag[rows])

    def reaching(side, nearest):
        return [d for d in offsets_of(nearest) if (d > 0) == (side == 0)]

    starts = (2 * G, 0)
    for at, side in enumerate(sides):
        for begin in range(0, k2, k1):
            lanes = pl.ds(begin, k1)
            sums = translated(
                top_table, top_pad.at[side], reaching(side, 2), starts[side], G, lanes
            )
            for part in range(2):
                known = top_edge[part, side * G : (side + 1) * G, lanes]
                top_sum[part, at * G : (at + 1) * G, lanes] = known + sums[part]

    leaf_sums = []
    for side in sides:
        window = both(pl.ds(HALO - PAD if side == 0 else HALO, PAD)).astype(BF16)
        patterns = mm(window, matrix[...])
        rows = slice(G, 2 * G) if side == 0 else slice(0, G)
        store_patterns(
            leaf_pad.at[side], pl.ds(G, G), slice(None), patterns[rows, :k1], patterns[rows, k1:]
        )
        leaf_sums.append(
            translated(
                leaf_table,
                leaf_pad.at[side],
                reaching(side, NEAR + 1),
                starts[side],
                G,
                pl.ds(0, k1),
            )
        )

    near_sums = []
    for side in sides:
        for part in range(2):
            near_pad[side, part] = jnp.zeros((4 * G, k1), F32)
            if side == 0:
                near_pad[0, part, G : 2 * G, :] = halo[part, HALO - G : HALO, :]
            else:
                near_pad[1, part, 3 * G :, :] = halo[part, HALO : HALO + G, :]
        total = jnp.zeros((PAD, 2 * k1), F32)
        for offset in range(1, NEAR + 1):
            start = 2 * G - offset if side == 0 else G + offset
            signed = offset if side == 0 else -offset
            total += mm(cells(near_pad.at[side], pl.ds(start, PAD)), near[NEAR + signed])
        near_sums.append(total)

    size = len(sides) * HALO
    back = disaggregated(
        top_sum,
        0,
        wide,
        weights,
        cosine,
        sine,
        edge_high.at[0 : 2 * size],
        edge_low.at[0 : 2 * size],
    )
    for at, side in enumerate(sides):
        blank = jnp.zeros((HALO - G, k1), F32)
        parts = []
        for part in range(2):
            extra = [leaf_sums[at][part], blank]
            extra = jnp.concatenate(extra if side == 0 else extra[::-1], axis=0)
            known = leaf_edge[part, rows_of[at], :]
            parts.append(
                (known + extra + back[part][at * HALO : (at + 1) * HALO]).astype(BF16)
            )
        blank = jnp.zeros((HALO - PAD, 2 * k1), F32)
        extra = [near_sums[at], blank]
        extra = jnp.concatenate(extra if side == 0 else extra[::-1], axis=0)
        total = mm_t(jnp.concatenate(parts, axis=1), matrix[...])
        total = total + near_edge[rows_of[at], :] + extra
        keep = live_edge[rows_of[at], :] == 1
        for part in range(2):
            values = total[:, part * k1 : (part + 1) * k1]
            fields[at][part] = jnp.where(keep, values, 0.0).astype(BF16)


def shards(
    currents,
    live_slots,
    radiation,
    near_tiles,
    leaf_transfer,
    top_transfer,
    interpolation,
    shift_angle,
):
    count = currents.shape[1]
    k1 = radiation.shape[2]
    k2 = interpolation.shape[1]
    parents = count // G
    offsets = 2 * REACH + 1
    edge = 2 * HALO
    axis = ("grp", "clu")
    region = lax.axis_size("clu")
    devices = lax.axis_size(axis)
    shape = jax.ShapeDtypeStruct
    hbm = pl.BlockSpec(memory_space=pltpu.HBM)
    vmem = pl.BlockSpec(memory_space=pltpu.VMEM)
    arrays = (
        currents,
        live_slots,
        radiation,
        near_tiles,
        jnp.swapaxes(leaf_transfer, 0, 1),
        jnp.swapaxes(top_transfer, 0, 1),
        interpolation,
        shift_angle,
    )
    arrays = [pltpu.with_memory_space_constraint(a, pltpu.HBM) for a in arrays]
    state = (
        shape((2, count - edge, k1), BF16),
        shape((edge, 2 * k1), F32),
        shape((2, edge, k1), F32),
        shape((2, 2 * G, k2), F32),
        shape((edge, k1), jnp.int32),
        shape((2 * k1, 2 * k1), BF16),
        shape((2 * NEAR + 1, 2 * k1, 2 * k1), BF16),
        shape((2 * k1, k2), BF16),
        shape((G, k2), F32),
        shape((G, k2), F32),
        shape((2, 2 * k1, 2 * k2), BF16),
        shape((offsets, 3, G, k1), F32),
        shape((offsets, 3, G, k2), F32),
    )
    local_scratch = [pltpu.VMEM(a.shape, a.dtype) for a in arrays] + [
        pltpu.SemaphoreType.DMA((len(arrays),)),
        pltpu.VMEM((2, count + 2 * PAD, k1), F32),
        pltpu.VMEM((3, count + 2 * PAD, k1), F32),
        pltpu.VMEM((3, parents + 2 * PAD, k2), F32),
        pltpu.VMEM((2, parents, k2), F32),
        pltpu.VMEM((2 * (count - edge), k2), BF16),
        pltpu.VMEM((2 * (count - edge), k2), BF16),
        pltpu.VMEM((2, count, k1), F32),
    ]
    send = shape((2, HALO, k1), BF16)
    params = pltpu.CompilerParams(vmem_limit_bytes=24 * 1024 * 1024)
    send_lead, *kept = pl.pallas_call(
        lead_kernel,
        out_shape=(send,) + state,
        in_specs=[hbm] * len(arrays),
        out_specs=(vmem,) * (1 + len(state)),
        scratch_shapes=[pltpu.VMEM((HALO, k1), jnp.int32), pltpu.SemaphoreType.DMA((2,))]
        + local_scratch,
        compiler_params=params,
        cost_estimate=pl.CostEstimate(flops=10**9, bytes_accessed=4*10**6, transcendentals=8192),
        name="lead_local",
    )(*arrays)

    def swaps(values, begin, keep):
        pairs = [(i, i + 1) for i in range(begin, devices - 1, 2) if keep(i)]
        return lax.ppermute(values, axis, pairs + [(j, i) for i, j in pairs])

    def leading(i):
        return i > 0 and i % region == 0

    inner = swaps(send_lead, 0, leading)
    outer_scratch = [
        pltpu.VMEM((2, edge, k1), F32),
        pltpu.VMEM((2, 2, 4 * G, k1), F32),
        pltpu.VMEM((2, 3, 3 * G, k1), F32),
        pltpu.VMEM((2, 3, 3 * G, k2), F32),
        pltpu.VMEM((2, 2 * G, k2), F32),
        pltpu.VMEM((2 * edge, k2), BF16),
        pltpu.VMEM((2 * edge, k2), BF16),
    ]
    near_cells = [pltpu.with_memory_space_constraint(a, pltpu.VMEM) for a in (currents, live_slots)]
    inner_rows = pl.pallas_call(
        inner_kernel,
        out_shape=send,
        in_specs=[vmem] * (3 + len(state)),
        out_specs=vmem,
        scratch_shapes=outer_scratch,
        compiler_params=params,
        cost_estimate=pl.CostEstimate(flops=0, bytes_accessed=0, transcendentals=0),
        name="inner_side",
    )(inner, *kept, *near_cells)
    send_cross, send_inner = pl.pallas_call(
        edge_kernel,
        out_shape=(send, send),
        in_specs=[vmem] * 3,
        out_specs=(vmem,) * 2,
        compiler_params=params,
        name="edges",
    )(*near_cells, inner_rows)
    cross = swaps(send_cross, 1, lambda i: True)
    inner_late = swaps(send_inner, 0, lambda i: not leading(i))
    return pl.pallas_call(
        last_kernel,
        out_shape=shape(currents.shape, BF16),
        in_specs=[hbm] * len(arrays) + [vmem] * (4 + len(state)),
        out_specs=hbm,
        scratch_shapes=[pltpu.VMEM(a.shape, a.dtype) for a in state]
        + local_scratch
        + [pltpu.VMEM(send.shape, BF16)] * 2
        + [pltpu.SemaphoreType.DMA((3,))]
        + outer_scratch,
        compiler_params=params,
        name="late_local_and_halo",
    )(*arrays, cross, inner, inner_late, inner_rows, *kept)


def solution(mesh):
    in_specs = (
        P(None, ("grp", "clu"), None),
        P(("grp", "clu"), None),
        P(),
        P(),
        P(),
        P(),
        P(),
        P(),
    )
    out_specs = P(None, ("grp", "clu"), None)
    return jax.shard_map(shards, mesh=mesh, in_specs=in_specs, out_specs=out_specs, check_vma=False)
```

```python
import math

import jax
import jax.numpy as jnp
from jax import lax
from jax.experimental import pallas as pl
from jax.experimental.pallas import tpu as pltpu
from jax.sharding import PartitionSpec as P

G = 8
NEAR = 2
REACH = 2 * G - 1
HALO = G * G
PAD = 2 * G
F32 = jnp.float32
BF16 = jnp.bfloat16


def split(values):
    high = values.astype(BF16)
    return high, (values - high.astype(F32)).astype(BF16)


def paired(real, imag):
    return jnp.concatenate(
        [jnp.concatenate([real, imag], axis=1), jnp.concatenate([-imag, real], axis=1)], axis=0
    )


def mm(left, right):
    return jnp.dot(left, right, preferred_element_type=F32)


def mm_t(left, right):
    return lax.dot_general(left, right, (((1,), (1,)), ((), ())), preferred_element_type=F32)


def cells(x, rows):
    return jnp.concatenate([x[0, rows, :], x[1, rows, :]], axis=1).astype(BF16)


def fill_table(table, transfer, nearest):
    width = transfer.shape[2]
    child = lax.broadcasted_iota(jnp.int32, (G, width), 0)
    for offset in range(-REACH, REACH + 1):
        if abs(offset) < nearest:
            continue
        index = offset + REACH
        real = jnp.broadcast_to(transfer[index, 0:1, :], (G, width))
        imag = jnp.broadcast_to(transfer[index, 1:2, :], (G, width))
        if offset > G:
            keep = child >= offset - G
        elif offset < -G:
            keep = child <= offset + REACH
        else:
            keep = None
        for part, value in enumerate((real, imag)):
            table[index, part] = value if keep is None else jnp.where(keep, value, 0.0)


def translated(table, patterns, offsets, start, rows, lanes):
    tiles = (rows // G, G, lanes.size)
    real = jnp.zeros(tiles, F32)
    imag = jnp.zeros(tiles, F32)
    for offset in offsets:
        pr, pi = [patterns[q, pl.ds(start - offset, rows), lanes].reshape(tiles) for q in range(2)]
        tr, ti = [table[offset + REACH, q, :, lanes][None] for q in range(2)]
        real += tr * pr - ti * pi
        imag += tr * pi + ti * pr
    return real.reshape(rows, lanes.size), imag.reshape(rows, lanes.size)


def offsets_of(nearest):
    return [d for d in range(-REACH, REACH + 1) if abs(d) >= nearest]


def store_patterns(patterns, rows, lanes, real, imag):
    patterns[0, rows, lanes] = real
    patterns[1, rows, lanes] = imag


def aggregated(by_child, parents, weights, cosine, sine, store):
    k1, k2 = weights.shape[0] // 2, weights.shape[1]
    stacked = jnp.concatenate([by_child[:, :k1], by_child[:, k1:]], axis=0)
    high, low = split(stacked)
    both = jnp.concatenate([high, low], axis=1)
    step = 256
    for begin in range(0, k2, step):
        cols = slice(begin, begin + step)
        int_high = weights[:k1, cols]
        twice = jnp.concatenate([int_high, int_high], axis=0)
        spread = mm(both, twice) + mm(high, weights[k1:, cols])
        real = jnp.zeros((parents, step), F32)
        imag = jnp.zeros((parents, step), F32)
        for c in range(G):
            sr = spread[c * parents : (c + 1) * parents]
            si = spread[(G + c) * parents : (G + c + 1) * parents]
            cc = cosine[c : c + 1, cols]
            ss = sine[c : c + 1, cols]
            real += cc * sr - ss * si
            imag += cc * si + ss * sr
        store(cols, real, imag)


def disaggregated(top_in, first, parents, weights, cosine, sine, spread_high, spread_low):
    k1, k2 = weights.shape[0] // 2, weights.shape[1]
    rows_each = parents * G
    for pair in range(0, parents, 2):
        reals, imags = [], []
        for p in (first + pair, first + pair + 1):
            tr = jnp.broadcast_to(top_in[0, p : p + 1, :], (G, k2))
            ti = jnp.broadcast_to(top_in[1, p : p + 1, :], (G, k2))
            reals.append(cosine[...] * tr + sine[...] * ti)
            imags.append(cosine[...] * ti - sine[...] * tr)
        for part, values in ((0, reals), (1, imags)):
            high, low = split(jnp.concatenate(values, axis=0))
            rows = pl.ds(part * rows_each + pair * G, 2 * G)
            spread_high[rows, :] = high
            spread_low[rows, :] = low
    wide = mm_t(spread_high[...], weights[...])
    back = wide[:, :k1] + wide[:, k1:] + mm_t(spread_low[...], weights[:k1])
    back = back * math.sqrt(k1 / k2)
    return back[:rows_each], back[rows_each:]


def local_part(inputs, state, work):
    hbm, staged, sems = inputs
    copies = [pltpu.make_async_copy(a, b, sems.at[i]) for i, (a, b) in enumerate(zip(hbm, staged))]
    for copy in copies:
        copy.start()
    for copy in copies:
        copy.wait()
    currents, live, radiation, tiles, leaf_transfer, top_transfer, interpolation, angle = staged
    (
        middle,
        near_edge,
        leaf_edge,
        top_edge,
        live_edge,
        matrix,
        near,
        weights,
        cosine,
        sine,
        combined,
        leaf_table,
        top_table,
    ) = state
    x, leaf_pat, top_pat, top_in, spread_high, spread_low, incoming = work
    count = currents.shape[1]
    k1 = radiation.shape[2]
    k2 = interpolation.shape[1]
    parents = count // G
    keep = live[...] == 1
    for part in range(2):
        x[part, 0:PAD, :] = jnp.zeros((PAD, k1), F32)
        x[part, PAD : PAD + count, :] = jnp.where(keep, currents[part].astype(F32), 0.0)
        x[part, PAD + count :, :] = jnp.zeros((PAD, k1), F32)
    live_edge[0:HALO] = live[0:HALO]
    live_edge[HALO:] = live[count - HALO :]
    fill_table(leaf_table, leaf_transfer, NEAR + 1)
    fill_table(top_table, top_transfer, 2)
    matrix[...] = paired(radiation[0], radiation[1])
    for index in range(2 * NEAR + 1):
        near[index] = paired(tiles[0, index], tiles[1, index])
    int_high, int_low = split(interpolation[...])
    weights[:k1] = int_high
    weights[k1:] = int_low
    cosine[...] = jnp.cos(angle[...])
    sine[...] = jnp.sin(angle[...])
    for part in range(2):
        half = matrix[:, part * k1 : (part + 1) * k1]
        high, low = split(mm(half, int_high) + mm(half, int_low))
        combined[0, :, part * k2 : (part + 1) * k2] = high
        combined[1, :, part * k2 : (part + 1) * k2] = low

    natural = mm(cells(x, pl.ds(0, count + 2 * PAD)), matrix[...])
    store_patterns(leaf_pat, slice(None), slice(None), natural[:, :k1], natural[:, k1:])
    ordered = [cells(x, pl.ds(PAD + c, parents, stride=G)) for c in range(G)]
    by_child = mm(jnp.concatenate(ordered, axis=0), matrix[...])

    def store(cols, real, imag):
        store_patterns(top_pat, pl.ds(PAD, parents), cols, real, imag)

    aggregated(by_child, parents, weights, cosine, sine, store)
    for part in range(2):
        top_pat[part, 0:PAD, :] = jnp.zeros((PAD, k2), F32)
        top_pat[part, PAD + parents :, :] = jnp.zeros((PAD, k2), F32)
    for begin in range(0, k2, k1):
        lanes = pl.ds(begin, k1)
        sums = translated(top_table, top_pat, offsets_of(2), PAD, parents, lanes)
        for part in range(2):
            top_in[part, :, lanes] = sums[part]
            top_edge[part, 0:G, lanes] = sums[part][:G]
            top_edge[part, G:, lanes] = sums[part][parents - G :]
    block = 4 * G
    for begin in range(0, count, block):
        sums = translated(
            leaf_table, leaf_pat, offsets_of(NEAR + 1), PAD + begin, block, pl.ds(0, k1)
        )
        for part in range(2):
            incoming[part, begin : begin + block, :] = sums[part]
    for part in range(2):
        leaf_edge[part, 0:HALO] = incoming[part, 0:HALO]
        leaf_edge[part, HALO:] = incoming[part, count - HALO :]

    total = jnp.zeros((count, 2 * k1), F32)
    for offset in range(-NEAR, NEAR + 1):
        total += mm(cells(x, pl.ds(PAD - offset, count)), near[offset + NEAR])
    near_edge[0:HALO] = total[:HALO]
    near_edge[HALO:] = total[count - HALO :]

    inside = slice(HALO, count - HALO)
    back = disaggregated(
        top_in, G, parents - 2 * G, weights, cosine, sine, spread_high, spread_low
    )
    gathered = jnp.concatenate(
        [(incoming[part, inside] + back[part]).astype(BF16) for part in range(2)], axis=1
    )
    field = mm_t(gathered, matrix[...]) + total[inside]
    for part in range(2):
        values = field[:, part * k1 : (part + 1) * k1]
        middle[part] = jnp.where(keep[inside], values, 0.0).astype(BF16)


def position():
    clu = lax.axis_index("clu")
    leads = jnp.logical_and(clu == 0, lax.axis_index("grp") > 0)
    return lax.rem(clu, 2), leads


def lead_kernel(*refs):
    hbm, send, state = refs[:8], refs[8], refs[9:22]
    alive, edge_sems = refs[22:24]
    staged, sems, work = refs[24:32], refs[32], refs[33:]
    odd, leads = position()

    @pl.when(jnp.logical_and(lax.axis_index("clu") < 2, lax.axis_index("grp") > 0))
    def _():
        currents, live = hbm[:2]
        begin = (1 - odd) * (currents.shape[1] - HALO)
        rows = pl.ds(pl.multiple_of(begin, HALO), HALO)
        copies = [
            pltpu.make_async_copy(currents.at[:, rows, :], send, edge_sems.at[0]),
            pltpu.make_async_copy(live.at[rows, :], alive, edge_sems.at[1]),
        ]
        for copy in copies:
            copy.start()
        for copy in copies:
            copy.wait()
        mask(send, send, alive[...])

    @pl.when(leads)
    def _():
        local_part((hbm, staged, sems), state, work)


def mask(target, source, alive):
    for part in range(2):
        target[part] = jnp.where(alive == 1, source[part].astype(F32), 0.0).astype(BF16)


def edge_kernel(currents, live, after, cross, inner):
    odd, _ = position()
    begin = currents.shape[1] - HALO
    for target, side in ((cross, odd), (inner, 1 - odd)):
        rows = pl.ds(pl.multiple_of(side * begin, HALO), HALO)
        mask(target, currents.at[:, rows, :], live[rows, :])


def inner_kernel(*refs):
    inner, state, rows = refs[0], refs[1:14], refs[16]
    halo, *work = refs[17:]
    odd, leads = position()

    @pl.when(leads)
    def _():
        for part in range(2):
            halo[part, HALO:, :] = inner[part].astype(F32)
        outer_part(halo, (1,), state, (rows,), work)


def last_kernel(*refs):
    hbm = refs[:8]
    cross, inner, inner_late, inner_rows = refs[8:12]
    state = refs[12:25]
    field = refs[25]
    late_state = refs[26:39]
    staged, sems, local_work = refs[39:47], refs[47], refs[48:55]
    lower, upper, out_sems, halo, *work = refs[55:]
    count = field.shape[1]
    inside = pl.ds(HALO, count - 2 * HALO)
    head, tail = pl.ds(0, HALO), pl.ds(count - HALO, HALO)
    odd, leads = position()

    def sent(source, rows, index):
        copy = pltpu.make_async_copy(source, field.at[:, rows, :], out_sems.at[index])
        copy.start()
        return copy

    @pl.when(leads)
    def _():
        copies = [sent(state[0], inside, 0), sent(inner_rows, tail, 1)]
        for part in range(2):
            halo[part, 0:HALO, :] = cross[part].astype(F32)
        outer_part(halo, (0,), state, (lower,), work)
        copies.append(sent(lower, head, 2))
        for copy in copies:
            copy.wait()

    @pl.when(jnp.logical_not(leads))
    def _():
        local_part((hbm, staged, sems), late_state, local_work)
        copies = [sent(late_state[0], inside, 0)]
        for part in range(2):
            halo[part, pl.ds(pl.multiple_of(odd * HALO, HALO), HALO), :] = cross[part].astype(F32)
            halo[part, pl.ds(pl.multiple_of((1 - odd) * HALO, HALO), HALO), :] = inner[
                part
            ].astype(F32) + inner_late[part].astype(F32)
        outer_part(halo, (0, 1), late_state, (lower, upper), work)
        copies += [sent(upper, tail, 1), sent(lower, head, 2)]
        for copy in copies:
            copy.wait()


def outer_part(halo, sides, state, fields, work):
    (
        middle,
        near_edge,
        leaf_edge,
        top_edge,
        live_edge,
        matrix,
        near,
        weights,
        cosine,
        sine,
        combined,
        leaf_table,
        top_table,
    ) = state
    near_pad, leaf_pad, top_pad, top_sum, edge_high, edge_low = work
    k1 = matrix.shape[0] // 2
    k2 = weights.shape[1]
    rows_of = [slice(side * HALO, (side + 1) * HALO) for side in sides]
    wide = len(sides) * G

    def both(rows):
        return jnp.concatenate([halo[0, rows, :], halo[1, rows, :]], axis=1)

    ordered = [both(pl.ds(side * HALO + c, G, stride=G)) for c in range(G) for side in sides]
    ordered = jnp.concatenate(ordered, axis=0).astype(BF16)
    for part in range(2):
        for side in sides:
            for begin in (0, 2 * G):
                top_pad[side, part, begin : begin + G, :] = jnp.zeros((G, k2), F32)
                leaf_pad[side, part, begin : begin + G, :] = jnp.zeros((G, k1), F32)
    step = 256
    for begin in range(0, k2, step):
        cols = slice(begin, begin + step)
        spread = []
        for first in (begin, k2 + begin):
            taken = slice(first, first + step)
            spread.append(mm(ordered, combined[0, :, taken]) + mm(ordered, combined[1, :, taken]))
        real = jnp.zeros((wide, step), F32)
        imag = jnp.zeros((wide, step), F32)
        for c in range(G):
            sr, si = [value[c * wide : (c + 1) * wide] for value in spread]
            cc = cosine[c : c + 1, cols]
            ss = sine[c : c + 1, cols]
            real += cc * sr - ss * si
            imag += cc * si + ss * sr
        for at, side in enumerate(sides):
            rows = slice(at * G, (at + 1) * G)
            store_patterns(top_pad.at[side], pl.ds(G, G), cols, real[rows], imag[rows])

    def reaching(side, nearest):
        return [d for d in offsets_of(nearest) if (d > 0) == (side == 0)]

    starts = (2 * G, 0)
    for at, side in enumerate(sides):
        for begin in range(0, k2, k1):
            lanes = pl.ds(begin, k1)
            sums = translated(
                top_table, top_pad.at[side], reaching(side, 2), starts[side], G, lanes
            )
            for part in range(2):
                known = top_edge[part, side * G : (side + 1) * G, lanes]
                top_sum[part, at * G : (at + 1) * G, lanes] = known + sums[part]

    leaf_sums = []
    for side in sides:
        window = both(pl.ds(HALO - PAD if side == 0 else HALO, PAD)).astype(BF16)
        patterns = mm(window, matrix[...])
        rows = slice(G, 2 * G) if side == 0 else slice(0, G)
        store_patterns(
            leaf_pad.at[side], pl.ds(G, G), slice(None), patterns[rows, :k1], patterns[rows, k1:]
        )
        leaf_sums.append(
            translated(
                leaf_table,
                leaf_pad.at[side],
                reaching(side, NEAR + 1),
                starts[side],
                G,
                pl.ds(0, k1),
            )
        )

    near_sums = []
    for side in sides:
        for part in range(2):
            near_pad[side, part] = jnp.zeros((4 * G, k1), F32)
            if side == 0:
                near_pad[0, part, G : 2 * G, :] = halo[part, HALO - G : HALO, :]
            else:
                near_pad[1, part, 3 * G :, :] = halo[part, HALO : HALO + G, :]
        total = jnp.zeros((PAD, 2 * k1), F32)
        for offset in range(1, NEAR + 1):
            start = 2 * G - offset if side == 0 else G + offset
            signed = offset if side == 0 else -offset
            total += mm(cells(near_pad.at[side], pl.ds(start, PAD)), near[NEAR + signed])
        near_sums.append(total)

    size = len(sides) * HALO
    back = disaggregated(
        top_sum,
        0,
        wide,
        weights,
        cosine,
        sine,
        edge_high.at[0 : 2 * size],
        edge_low.at[0 : 2 * size],
    )
    for at, side in enumerate(sides):
        blank = jnp.zeros((HALO - G, k1), F32)
        parts = []
        for part in range(2):
            extra = [leaf_sums[at][part], blank]
            extra = jnp.concatenate(extra if side == 0 else extra[::-1], axis=0)
            known = leaf_edge[part, rows_of[at], :]
            parts.append(
                (known + extra + back[part][at * HALO : (at + 1) * HALO]).astype(BF16)
            )
        blank = jnp.zeros((HALO - PAD, 2 * k1), F32)
        extra = [near_sums[at], blank]
        extra = jnp.concatenate(extra if side == 0 else extra[::-1], axis=0)
        total = mm_t(jnp.concatenate(parts, axis=1), matrix[...])
        total = total + near_edge[rows_of[at], :] + extra
        keep = live_edge[rows_of[at], :] == 1
        for part in range(2):
            values = total[:, part * k1 : (part + 1) * k1]
            fields[at][part] = jnp.where(keep, values, 0.0).astype(BF16)


def shards(
    currents,
    live_slots,
    radiation,
    near_tiles,
    leaf_transfer,
    top_transfer,
    interpolation,
    shift_angle,
):
    count = currents.shape[1]
    k1 = radiation.shape[2]
    k2 = interpolation.shape[1]
    parents = count // G
    offsets = 2 * REACH + 1
    edge = 2 * HALO
    axis = ("grp", "clu")
    region = lax.axis_size("clu")
    devices = lax.axis_size(axis)
    shape = jax.ShapeDtypeStruct
    hbm = pl.BlockSpec(memory_space=pltpu.HBM)
    vmem = pl.BlockSpec(memory_space=pltpu.VMEM)
    arrays = (
        currents,
        live_slots,
        radiation,
        near_tiles,
        jnp.swapaxes(leaf_transfer, 0, 1),
        jnp.swapaxes(top_transfer, 0, 1),
        interpolation,
        shift_angle,
    )
    arrays = [pltpu.with_memory_space_constraint(a, pltpu.HBM) for a in arrays]
    state = (
        shape((2, count - edge, k1), BF16),
        shape((edge, 2 * k1), F32),
        shape((2, edge, k1), F32),
        shape((2, 2 * G, k2), F32),
        shape((edge, k1), jnp.int32),
        shape((2 * k1, 2 * k1), BF16),
        shape((2 * NEAR + 1, 2 * k1, 2 * k1), BF16),
        shape((2 * k1, k2), BF16),
        shape((G, k2), F32),
        shape((G, k2), F32),
        shape((2, 2 * k1, 2 * k2), BF16),
        shape((offsets, 2, G, k1), F32),
        shape((offsets, 2, G, k2), F32),
    )
    local_scratch = [pltpu.VMEM(a.shape, a.dtype) for a in arrays] + [
        pltpu.SemaphoreType.DMA((len(arrays),)),
        pltpu.VMEM((2, count + 2 * PAD, k1), F32),
        pltpu.VMEM((2, count + 2 * PAD, k1), F32),
        pltpu.VMEM((2, parents + 2 * PAD, k2), F32),
        pltpu.VMEM((2, parents, k2), F32),
        pltpu.VMEM((2 * (count - edge), k2), BF16),
        pltpu.VMEM((2 * (count - edge), k2), BF16),
        pltpu.VMEM((2, count, k1), F32),
    ]
    send = shape((2, HALO, k1), BF16)
    params = pltpu.CompilerParams(vmem_limit_bytes=24 * 1024 * 1024)
    send_lead, *kept = pl.pallas_call(
        lead_kernel,
        out_shape=(send,) + state,
        in_specs=[hbm] * len(arrays),
        out_specs=(vmem,) * (1 + len(state)),
        scratch_shapes=[pltpu.VMEM((HALO, k1), jnp.int32), pltpu.SemaphoreType.DMA((2,))]
        + local_scratch,
        compiler_params=params,
        cost_estimate=pl.CostEstimate(flops=10**9, bytes_accessed=4*10**6, transcendentals=8192),
        name="lead_local",
    )(*arrays)

    def swaps(values, begin, keep):
        pairs = [(i, i + 1) for i in range(begin, devices - 1, 2) if keep(i)]
        return lax.ppermute(values, axis, pairs + [(j, i) for i, j in pairs])

    def leading(i):
        return i > 0 and i % region == 0

    inner = swaps(send_lead, 0, leading)
    outer_scratch = [
        pltpu.VMEM((2, edge, k1), F32),
        pltpu.VMEM((2, 2, 4 * G, k1), F32),
        pltpu.VMEM((2, 2, 3 * G, k1), F32),
        pltpu.VMEM((2, 2, 3 * G, k2), F32),
        pltpu.VMEM((2, 2 * G, k2), F32),
        pltpu.VMEM((2 * edge, k2), BF16),
        pltpu.VMEM((2 * edge, k2), BF16),
    ]
    near_cells = [pltpu.with_memory_space_constraint(a, pltpu.VMEM) for a in (currents, live_slots)]
    inner_rows = pl.pallas_call(
        inner_kernel,
        out_shape=send,
        in_specs=[vmem] * (3 + len(state)),
        out_specs=vmem,
        scratch_shapes=outer_scratch,
        compiler_params=params,
        cost_estimate=pl.CostEstimate(flops=0, bytes_accessed=0, transcendentals=0),
        name="inner_side",
    )(inner, *kept, *near_cells)
    send_cross, send_inner = pl.pallas_call(
        edge_kernel,
        out_shape=(send, send),
        in_specs=[vmem] * 3,
        out_specs=(vmem,) * 2,
        compiler_params=params,
        name="edges",
    )(*near_cells, inner_rows)
    cross = swaps(send_cross, 1, lambda i: True)
    inner_late = swaps(send_inner, 0, lambda i: not leading(i))
    return pl.pallas_call(
        last_kernel,
        out_shape=shape(currents.shape, BF16),
        in_specs=[hbm] * len(arrays) + [vmem] * (4 + len(state)),
        out_specs=hbm,
        scratch_shapes=[pltpu.VMEM(a.shape, a.dtype) for a in state]
        + local_scratch
        + [pltpu.VMEM(send.shape, BF16)] * 2
        + [pltpu.SemaphoreType.DMA((3,))]
        + outer_scratch,
        compiler_params=params,
        name="late_local_and_halo",
    )(*arrays, cross, inner, inner_late, inner_rows, *kept)


def solution(mesh):
    in_specs = (
        P(None, ("grp", "clu"), None),
        P(("grp", "clu"), None),
        P(),
        P(),
        P(),
        P(),
        P(),
        P(),
    )
    out_specs = P(None, ("grp", "clu"), None)
    return jax.shard_map(shards, mesh=mesh, in_specs=in_specs, out_specs=out_specs, check_vma=False)
```
